32 devices in a mesh: parts: 2 (over y), lat: 4 (over z), height: 2 (over x), sub: 2 (over core).
Axes of the slice: x: 2, y: 2, z: 4, core: 2. Of those that a mesh axis runs over, the one named last changes fastest.
Arguments:
- thermal_excess_field: float32 [128, 16, 128], P(('parts', 'lat', 'sub'), 'height'), parts along dimension 0, may hold values from -6 to 6
- thermal_diffusivity: float32 [128, 16, 128], P(('parts', 'lat', 'sub'), 'height'), parts along dimension 0, may hold values from 0.1 to 0.9
- material_shift_field: float32 [3, 128, 16, 128], P(None, ('parts', 'lat', 'sub'), 'height'), parts along dimension 1, may hold values from -0.15 to 0.15
- stack_deposit_tally: int32 [128, 128], P('parts'), parts along dimension 0, may hold values from 4 to 16
- laser_target_sites: int32 [4, 128], P('parts'), parts along dimension 0, may hold values from 0 to 131071
Outputs:
- temperature_out: float32 [128, 16, 128], P(('parts', 'lat', 'sub'), 'height'), parts along dimension 0
- force: float32 [3, 128, 16, 128], P(None, ('parts', 'lat', 'sub'), 'height'), parts along dimension 1
The draws below stay inside these ranges and needn't reach their ends.
There are 2 independent parts, one for each index of `parts`. The reference program is written for one: setup_inputs(seed, part) draws one part's arguments, and reference() takes and returns one part's arrays. A program takes and returns all parts, laid end to end along the dimension named above; each array names one. Nothing has to cross between parts.
Inputs may be any that keep to these rules, and one draw needn't show every extreme that they name: stack_deposit_tally counts, for each column, the active points from the base of the build upward. laser_target_sites holds flat cell indices; an index may repeat.
All inputs are finite; a program needn't handle non-finite values.
Results may differ from the reference program's by a relative error of at most 0.00002.
Values sent between devices are 32-bit elements; how exact they have to be, the bound alone decides.
A program may use at most 64 MiB of HBM per device.

```python
import math
import jax
import jax.numpy as jnp
from jax import lax

HEAT_STEPS = 2
NODES_ACROSS = 64
NODES_VERTICAL = 16
NODES_SIDEWAYS = 128
SPOTS = 128


def with_ends(array, rng, smallest, largest):
    spot = [jax.random.randint(jax.random.fold_in(rng, axis), (), 0, length) for axis, length in enumerate(array.shape)]
    widest = array.shape.index(max(array.shape))
    beside = spot[:widest] + [(spot[widest] + 1) % array.shape[widest]] + spot[widest + 1:]
    return array.at[tuple(spot)].set(smallest).at[tuple(beside)].set(largest)


def level_of(rng, shape, cuts, low, high):
    def one(axis_at, shards_of):
        steps = jax.random.uniform(jax.random.fold_in(jax.random.fold_in(rng, 6), axis_at), (shards_of,), jnp.float32, low / len(cuts), high / len(cuts))
        return jnp.repeat(jnp.exp(steps), shape[axis_at] // shards_of).reshape((-1,) + (1,) * (len(shape) - axis_at - 1))

    level = one(*cuts[0])
    for cut in cuts[1:]:
        level = level * one(*cut)
    return level


def centred(rng, dims, width, bound, shards=(), held_as=jnp.bfloat16):
    values = jax.random.normal(rng, dims, jnp.float32) * width
    if len(shards) > 0:
        values = level_of(rng, dims, shards, -0.22, 0.18) * values
    return jnp.clip(values, min=-bound, max=bound).astype(held_as)


def setup_inputs(seed: int = 0, part: int = 0) -> dict:
    key_list = jax.random.split(jax.random.key(seed), 6)
    part_splits = jax.random.split(jax.random.fold_in(key_list[5], part), 6)
    return {
        "thermal_excess_field": centred(part_splits[0], (NODES_ACROSS, NODES_VERTICAL, NODES_SIDEWAYS), 1.0, 6.0, ((0, 8), (1, 2)), jnp.float32),
        "thermal_diffusivity": jnp.clip(jnp.exp(math.log(0.9) - 2.1972245 * jax.random.uniform(part_splits[1], (NODES_ACROSS, NODES_VERTICAL, NODES_SIDEWAYS), jnp.float32) ** level_of(part_splits[1], (NODES_ACROSS, NODES_VERTICAL, NODES_SIDEWAYS), ((0, 8), (1, 2)), -0.2, 0.2)), 0.1, 0.9),
        "material_shift_field": jnp.clip(jax.random.uniform(part_splits[2], (3, NODES_ACROSS, NODES_VERTICAL, NODES_SIDEWAYS), jnp.float32, -0.15, 0.15) * level_of(part_splits[2], (3, NODES_ACROSS, NODES_VERTICAL, NODES_SIDEWAYS), ((1, 8), (2, 2)), -0.4, 0.0), -0.15, 0.15),
        "stack_deposit_tally": with_ends(jax.random.randint(part_splits[3], (NODES_ACROSS, NODES_SIDEWAYS), max(2, NODES_VERTICAL // 4), NODES_VERTICAL + 1), jax.random.fold_in(part_splits[3], 1), max(2, NODES_VERTICAL // 4), NODES_VERTICAL).astype(jnp.int32),
        "laser_target_sites": with_ends(jax.random.randint(part_splits[4], (HEAT_STEPS, SPOTS), 0, NODES_ACROSS * NODES_VERTICAL * NODES_SIDEWAYS), jax.random.fold_in(part_splits[4], 1), 0, (NODES_ACROSS * NODES_VERTICAL * NODES_SIDEWAYS) - 1).astype(jnp.int32),
    }


laser_energy_input = 1.5
thermal_swelling = 0.01
pressure_coef = -10.0
stiffness_coef = 300.0

def bond_offsets():
    result = []
    for shift_one in range(-3, 4):
        for shift_two in range(-3, 4):
            for shift_three in range(-3, 4):
                radius = shift_one * shift_one + shift_two * shift_two + shift_three * shift_three
                if 0 < radius <= 9:
                    result.append([shift_one, shift_two, shift_three])
    return result

def border_extend_field(grid_field):
    widths = [(0, 0)] * (grid_field.ndim - 3) + [(3, 3), (3, 3), (3, 3)]
    return jnp.pad(grid_field, widths)

def translated_view(padded, neighbour_step):
    lead = [jnp.zeros((), jnp.int32)] * (padded.ndim - 3)
    starts = lead + [neighbour_step[0] + 3, neighbour_step[1] + 3, neighbour_step[2] + 3]
    sizes = list(padded.shape[:-3]) + [NODES_ACROSS, NODES_VERTICAL, NODES_SIDEWAYS]
    return lax.dynamic_slice(padded, starts, sizes)

def reference(thermal_excess_field, thermal_diffusivity, material_shift_field, stack_deposit_tally, laser_target_sites):
    neighbour_step_list = jnp.asarray(bond_offsets(), dtype=jnp.int32)
    offset_float = neighbour_step_list.astype(jnp.float32)
    separation_table = jnp.sqrt(lax.optimization_barrier(jnp.sum(offset_float * offset_float, axis=1)))
    influence_total = jnp.sum(1.0 / separation_table)
    heights = jnp.arange(NODES_VERTICAL, dtype=jnp.int32)
    solid_mask = (heights[None, :, None] < stack_deposit_tally[:, None, :]).astype(jnp.float32)
    solid_mask_bordered = border_extend_field(solid_mask)
    diffusivity_bordered = border_extend_field(thermal_diffusivity)
    present_thermal_field = thermal_excess_field
    for substep in range(HEAT_STEPS):
        laser_deposit_term = jnp.zeros((NODES_ACROSS * NODES_VERTICAL * NODES_SIDEWAYS,), jnp.float32).at[laser_target_sites[substep]].add(1.0).reshape(NODES_ACROSS, NODES_VERTICAL, NODES_SIDEWAYS)
        thermal_field_bordered = border_extend_field(present_thermal_field)

        def thermal_pair_link(running, bond_data):
            neighbour_step, separation = bond_data
            pair_contribution = translated_view(solid_mask_bordered, neighbour_step) * (thermal_diffusivity + translated_view(diffusivity_bordered, neighbour_step)) * (translated_view(thermal_field_bordered, neighbour_step) - present_thermal_field) * (0.5 / (influence_total * separation))
            return (running + pair_contribution, None)
        energy_flow_rate, discarded_output = lax.scan(thermal_pair_link, jnp.zeros_like(present_thermal_field), (neighbour_step_list, separation_table))
        present_thermal_field = present_thermal_field + solid_mask * (energy_flow_rate + laser_energy_input * laser_deposit_term)
    disp_pad = border_extend_field(material_shift_field)
    thermal_field_bordered = border_extend_field(present_thermal_field)

    def bond_state(neighbour_step, offset_vec, separation):
        near_u = translated_view(disp_pad, neighbour_step)
        deformed = [offset_vec[0] + near_u[0] - material_shift_field[0], offset_vec[1] + near_u[1] - material_shift_field[1], offset_vec[2] + near_u[2] - material_shift_field[2]]
        reach_extent = jnp.sqrt(deformed[0] * deformed[0] + deformed[1] * deformed[1] + deformed[2] * deformed[2])
        elongation_ratio = reach_extent - separation - thermal_swelling * (present_thermal_field + translated_view(thermal_field_bordered, neighbour_step)) * separation
        return (deformed, reach_extent, elongation_ratio)

    def volume_bond(running, bond_data):
        neighbour_step, offset_vec, separation = bond_data
        deformed, reach_extent, elongation_ratio = bond_state(neighbour_step, offset_vec, separation)
        near_a = translated_view(solid_mask_bordered, neighbour_step)
        return ((running[0] + near_a * separation, running[1] + near_a * elongation_ratio), None)
    zeros_grid = jnp.zeros((NODES_ACROSS, NODES_VERTICAL, NODES_SIDEWAYS), jnp.float32)
    sums, discarded_output = lax.scan(volume_bond, (zeros_grid, zeros_grid), (neighbour_step_list, offset_float, separation_table))
    volume = jnp.where(solid_mask > 0, sums[0], 1.0)
    dilatation = solid_mask * 3.0 * sums[1] / volume
    pressure = pressure_coef * dilatation / volume
    stiffness = stiffness_coef / volume
    pressure_pad = border_extend_field(pressure)
    stiffness_pad = border_extend_field(stiffness)

    def force_bond(running, bond_data):
        neighbour_step, offset_vec, separation = bond_data
        deformed, reach_extent, elongation_ratio = bond_state(neighbour_step, offset_vec, separation)
        near_a = translated_view(solid_mask_bordered, neighbour_step)
        scalar = near_a * (pressure + translated_view(pressure_pad, neighbour_step) + (stiffness + translated_view(stiffness_pad, neighbour_step)) * elongation_ratio / separation) / reach_extent
        return ((running[0] + scalar * deformed[0], running[1] + scalar * deformed[1], running[2] + scalar * deformed[2]), None)
    parts_sum, discarded_output = lax.scan(force_bond, (zeros_grid, zeros_grid, zeros_grid), (neighbour_step_list, offset_float, separation_table))
    traction_result = solid_mask[None] * jnp.stack(parts_sum)
    return (present_thermal_field, traction_result)
```

```python
import functools
import math

import jax
import jax.numpy as jnp
from jax import lax
from jax.experimental import pallas as pl
from jax.experimental.pallas import tpu as pltpu
from jax.sharding import PartitionSpec as P

laser_energy_input = 1.5
thermal_swelling = 0.01
pressure_coef = -10.0
stiffness_coef = 300.0

RIM = 3
REACH = RIM * RIM
BASE = 8

OFFSETS = [
    (a, b, c)
    for c in range(-RIM, RIM + 1)
    for a in range(-RIM, RIM + 1)
    for b in range(-RIM, RIM + 1)
    if 0 < a * a + b * b + c * c <= REACH
]
PLANE = [
    (a, b)
    for a in range(-RIM, RIM + 1)
    for b in range(-RIM, RIM + 1)
    if a * a + b * b <= REACH
]
SQUARES = sorted({a * a + b * b for a, b in PLANE})
TOTAL_WEIGHT = sum(1.0 / math.sqrt(a * a + b * b + c * c) for a, b, c in OFFSETS)
DIRECTIONS = [(dx, dz) for dx in (-1, 0, 1) for dz in (-1, 0, 1) if (dx, dz) != (0, 0)]
PHASE_FIELDS = (5, 2, 1, 1)


def inverse_distance(square):
    return 1.0 / math.sqrt(square)


def kernel(
    temp_in,
    cond_in,
    shift_in,
    tally_in,
    sites_in,
    temp_out,
    force_out,
    e1,
    e2,
    e3,
    e4,
    p1,
    p2,
    p3,
    p4,
    z1,
    z2,
    z3,
    z4,
    c1,
    c2,
    c3,
    c4,
    tally,
    sites,
    act,
    act_k,
    act_t,
    act_kt,
    source,
    sum_a,
    sum_ak,
    vol,
    dil,
    lean,
    total,
    normal,
    strain,
    local_sem,
    send_sem,
    recv_sem,
):
    nx, nz, lanes = temp_in.shape
    across_total = tally_in.shape[0]
    n_sub = lax.axis_size("sub")
    n_lateral = lax.axis_size("lat") * n_sub
    n_height = lax.axis_size("height")
    total_z = n_height * nz
    at_x = lax.axis_index("lat") * n_sub + lax.axis_index("sub")
    at_z = lax.axis_index("height")
    start_x = at_x * nx
    start_z = at_z * nz
    own_x = slice(RIM, RIM + nx)
    own_z = slice(BASE, BASE + nz)
    ext, packed, faces, corners = (e1, e2, e3, e4), (p1, p2, p3, p4), (z1, z2, z3, z4), (c1, c2, c3, c4)

    def exists(dx, dz):
        result = None
        for step, at, count in ((dx, at_x, n_lateral), (dz, at_z, n_height)):
            if step:
                test = at + step >= 0 if step < 0 else at + step < count
                result = test if result is None else jnp.logical_and(result, test)
        return result

    def device(dx, dz):
        to_x = at_x + dx
        return {"lat": to_x // n_sub, "sub": to_x % n_sub, "height": at_z + dz}

    def message(phase, which):
        dx, dz = DIRECTIONS[which]
        if dz == 0:
            here = slice(RIM, 2 * RIM) if dx < 0 else slice(nx, RIM + nx)
            there = slice(RIM + nx, 2 * RIM + nx) if dx < 0 else slice(0, RIM)
            src = ext[phase].at[:, here, own_z]
            dst = ext[phase].at[:, there, own_z]
        else:
            side, far = (0, 1) if dz < 0 else (1, 0)
            if dx == 0:
                src, dst = packed[phase].at[side], faces[phase].at[far]
            else:
                rows = slice(0, 16) if dx < 0 else slice(RIM * nx - 16, RIM * nx)
                src = packed[phase].at[side, :, rows]
                dst = corners[phase].at[far, 1 if dx < 0 else 0]
        return pltpu.make_async_remote_copy(
            src_ref=src,
            dst_ref=dst,
            send_sem=send_sem.at[phase, which],
            recv_sem=recv_sem.at[phase, which],
            device_id=device(dx, dz),
            device_id_type=pl.DeviceIdType.MESH,
        )

    def pack(phase):
        for f in range(PHASE_FIELDS[phase]):
            for x in range(nx):
                tile = ext[phase][f, RIM + x, own_z, :]
                packed[phase][0, f, RIM * x : RIM * x + RIM, :] = tile[0:RIM]
                packed[phase][1, f, RIM * x : RIM * x + RIM, :] = tile[nz - RIM : nz]

    def send(phase):
        for which, (dx, dz) in enumerate(DIRECTIONS):

            @pl.when(exists(dx, dz))
            def _(which=which):
                message(phase, which).start()

    def receive(phase):
        for which, (dx, dz) in enumerate(DIRECTIONS):

            @pl.when(exists(-dx, -dz))
            def _(which=which):
                message(phase, which).wait_recv()

        for f in range(PHASE_FIELDS[phase]):
            for side in range(2):
                rows = slice(BASE - RIM, BASE) if side == 0 else slice(BASE + nz, BASE + nz + RIM)
                for x in range(nx):
                    ext[phase][f, RIM + x, rows, :] = faces[phase][side, f, RIM * x : RIM * x + RIM, :]
                for i in range(RIM):
                    low = 16 - REACH + RIM * i
                    ext[phase][f, i, rows, :] = corners[phase][side, 0, f, low : low + RIM, :]
                    ext[phase][f, RIM + nx + i, rows, :] = corners[phase][
                        side, 1, f, RIM * i : RIM * i + RIM, :
                    ]

    loads = [
        pltpu.make_async_copy(temp_in, e1.at[0, own_x, own_z], local_sem.at[0]),
        pltpu.make_async_copy(cond_in, e1.at[1, own_x, own_z], local_sem.at[1]),
        pltpu.make_async_copy(shift_in, e1.at[2:5, own_x, own_z], local_sem.at[2]),
        pltpu.make_async_copy(tally_in, tally, local_sem.at[3]),
        pltpu.make_async_copy(sites_in, sites, local_sem.at[4]),
    ]
    for load in loads:
        load.start()

    for phase in range(4):
        for f in range(PHASE_FIELDS[phase]):
            zeros = jnp.zeros((RIM, nz, lanes), jnp.float32)
            ext[phase][f, 0:RIM, own_z, :] = zeros
            ext[phase][f, RIM + nx : 2 * RIM + nx, own_z, :] = zeros
        faces[phase][...] = jnp.zeros_like(faces[phase])
        corners[phase][...] = jnp.zeros_like(corners[phase])

    barrier = pltpu.get_barrier_semaphore()
    for dx, dz in DIRECTIONS:

        @pl.when(exists(dx, dz))
        def _(dx=dx, dz=dz):
            pl.semaphore_signal(
                barrier, inc=1, device_id=device(dx, dz), device_id_type=pl.DeviceIdType.MESH
            )

    for load in loads[:3]:
        load.wait()
    pack(0)
    beside = jnp.where(at_x > 0, 1, 0) + jnp.where(at_x + 1 < n_lateral, 1, 0)
    stacked = jnp.where(at_z > 0, 1, 0) + jnp.where(at_z + 1 < n_height, 1, 0)
    pl.semaphore_wait(barrier, (beside + 1) * (stacked + 1) - 1)

    send(0)

    lane = lax.broadcasted_iota(jnp.int32, (nz, lanes), 1)

    def frame(value, c):
        return value if c == 0 else pltpu.roll(value, c % lanes, 1)

    def unframe(value, c):
        if c == 0:
            return value
        inside = lane < lanes - c if c > 0 else lane >= -c
        return jnp.where(inside, pltpu.roll(value, (-c) % lanes, 1), 0.0)

    def near(ref, x, a, b):
        return ref[x + (RIM + a), BASE + b : BASE + b + nz, :]

    def ring_sums(ref, x):
        sums = {}
        for a, b in PLANE:
            square = a * a + b * b
            value = near(ref, x, a, b)
            sums[square] = sums[square] + value if square in sums else value
        return sums

    def weighted(sums, weight):
        result = None
        for c in range(RIM + 1):
            part = None
            for square in SQUARES:
                if 0 < square + c * c <= REACH:
                    term = sums[square] * weight(square + c * c)
                    part = term if part is None else part + term
            for sign in (1, -1) if c else (1,):
                moved = unframe(part, sign * c)
                result = moved if result is None else result + moved
        return result

    for load in loads[3:]:
        load.wait()
    heights = start_z - BASE + lax.broadcasted_iota(jnp.int32, (act.shape[1], lanes), 0)
    for x in range(nx + 2 * RIM):
        line = start_x + (x - RIM)
        count = tally[pl.ds(jnp.clip(line, 0, across_total - 1), 1), :]
        count = jnp.where(jnp.logical_and(line >= 0, line < across_total), count, 0)
        act[x] = jnp.where((heights >= 0) & (heights < count), 1.0, 0.0)

    for step in range(2):
        spots = sites[step : step + 1, :]
        n_spots = spots.shape[1]
        rows = []
        for x in range(nx):
            level = start_z + lax.broadcasted_iota(jnp.int32, (nz, n_spots), 0)
            gap = spots - ((start_x + x) * total_z + level) * lanes
            rows.append(jnp.where((gap >= 0) & (gap < lanes), 1.0, 0.0))
        row_hit = jnp.concatenate(rows, 0)
        lane_hit = jnp.where(
            lax.broadcasted_iota(jnp.int32, (lanes, n_spots), 0) == lax.rem(spots, lanes), 1.0, 0.0
        )
        hits = lax.dot_general(
            row_hit, lane_hit, (((1,), (1,)), ((), ())), preferred_element_type=jnp.float32
        )
        source[step] = hits.reshape(nx, nz, lanes)

    @pl.loop(0, nx)
    def _(x):
        sums = ring_sums(act, x)
        sum_a[x] = weighted(sums, inverse_distance)
        mass = weighted(sums, math.sqrt)
        mass = jnp.where(near(act, x, 0, 0) > 0, mass, 1.0)
        vol[x] = mass
        e2[1, x + RIM, own_z, :] = stiffness_coef / mass

    receive(0)

    def heat(field, step, x):
        rate_t = weighted(ring_sums(act_t, x), inverse_distance)
        rate_kt = weighted(ring_sums(act_kt, x), inverse_distance)
        temp = near(field, x, 0, 0)
        cond = near(e1.at[1], x, 0, 0)
        flow = cond * rate_t + rate_kt - temp * (cond * sum_a[x] + sum_ak[x])
        return temp + near(act, x, 0, 0) * (
            flow * (0.5 / TOTAL_WEIGHT) + laser_energy_input * source[step, x]
        )

    @pl.loop(0, nx + 2 * RIM)
    def _(x):
        act_k[x] = act[x] * e1[1, x]
        act_t[x] = act[x] * e1[0, x]
        act_kt[x] = act_k[x] * e1[0, x]

    @pl.loop(0, nx)
    def _(x):
        sum_ak[x] = weighted(ring_sums(act_k, x), inverse_distance)
        e2[0, x + RIM, own_z, :] = heat(e1.at[0], 0, x)

    pack(1)
    send(1)

    def geometry(x):
        centre = [near(e1.at[2 + k], x, 0, 0) for k in range(3)]
        stretched = None
        leaning = [None] * 3
        bond = 0
        for c in range(-RIM, RIM + 1):
            moved = [frame(value, c) for value in centre]
            first = {a: moved[0] - float(a) for a in range(-RIM, RIM + 1)}
            second = {b: moved[1] - float(b) for b in range(-RIM, RIM + 1)}
            third = moved[2] - float(c)
            part = None
            parts = [None] * 3
            for a, b, other in OFFSETS:
                if other != c:
                    continue
                separation = math.sqrt(a * a + b * b + c * c)
                d = (
                    near(e1.at[2], x, a, b) - first[a],
                    near(e1.at[3], x, a, b) - second[b],
                    near(e1.at[4], x, a, b) - third,
                )
                square = d[0] * d[0] + d[1] * d[1] + d[2] * d[2]
                inverse = lax.rsqrt(square)
                there = near(act, x, a, b)
                change = square * inverse - separation
                strain[x, bond] = change * (1.0 / separation)
                masked = inverse * there
                change = change * there
                part = change if part is None else part + change
                for k in range(3):
                    unit = d[k] * masked
                    normal[x, bond, k] = unit
                    parts[k] = unit if parts[k] is None else parts[k] + unit
                bond += 1
            part = unframe(part, c)
            stretched = part if stretched is None else stretched + part
            for k in range(3):
                leaned = unframe(parts[k], c)
                leaning[k] = leaned if leaning[k] is None else leaning[k] + leaned
        dil[x] = stretched
        for k in range(3):
            lean[k, x] = leaning[k]

    @pl.loop(0, nx)
    def _(x):
        geometry(x)

    receive(1)

    @pl.loop(0, nx + 2 * RIM)
    def _(x):
        act_t[x] = act[x] * e2[0, x]
        act_kt[x] = act_k[x] * e2[0, x]

    @pl.loop(0, nx)
    def _(x):
        e3[0, x + RIM, own_z, :] = heat(e2.at[0], 1, x)

    pack(2)
    send(2)
    store_temp = pltpu.make_async_copy(e3.at[0, own_x, own_z], temp_out, local_sem.at[0])
    store_temp.start()

    receive(2)

    @pl.loop(0, nx + 2 * RIM)
    def _(x):
        act_t[x] = act[x] * e3[0, x]

    @pl.loop(0, nx)
    def _(x):
        mass = vol[x]
        swell = weighted(ring_sums(act_t, x), math.sqrt) + near(e3.at[0], x, 0, 0) * mass
        change = near(act, x, 0, 0) * 3.0 * (dil[x] - thermal_swelling * swell) / mass
        e4[0, x + RIM, own_z, :] = pressure_coef * change / mass

    pack(3)
    send(3)

    @pl.loop(0, nx)
    def _(x):
        result = [None] * 3
        bond = 0
        for c in range(-RIM, RIM + 1):
            stiff = frame(near(e2.at[1], x, 0, 0), c)
            warm = frame(near(e3.at[0], x, 0, 0), c)
            parts = [None] * 3
            for a, b, other in OFFSETS:
                if other != c:
                    continue
                swell = (warm + near(e3.at[0], x, a, b)) * thermal_swelling
                scale = (stiff + near(e2.at[1], x, a, b)) * (strain[x, bond] - swell)
                for k in range(3):
                    term = normal[x, bond, k] * scale
                    parts[k] = term if parts[k] is None else parts[k] + term
                bond += 1
            for k in range(3):
                moved = unframe(parts[k], c)
                result[k] = moved if result[k] is None else result[k] + moved
        for k in range(3):
            total[k, x] = result[k]

    receive(3)

    @pl.loop(0, nx)
    def _(x):
        pressure = near(e4.at[0], x, 0, 0)
        result = [total[k, x] + pressure * lean[k, x] for k in range(3)]
        bond = 0
        for c in range(-RIM, RIM + 1):
            parts = [None] * 3
            for a, b, other in OFFSETS:
                if other != c:
                    continue
                push = near(e4.at[0], x, a, b)
                for k in range(3):
                    term = normal[x, bond, k] * push
                    parts[k] = term if parts[k] is None else parts[k] + term
                bond += 1
            for k in range(3):
                result[k] = result[k] + unframe(parts[k], c)
        for k in range(3):
            force_out[k, x] = near(act, x, 0, 0) * result[k]

    store_temp.wait()
    for phase in range(4):
        for which, (dx, dz) in enumerate(DIRECTIONS):

            @pl.when(exists(dx, dz))
            def _(phase=phase, which=which):
                message(phase, which).wait_send()


def per_device(temp, cond, shift, tally, sites):
    nx, nz, lanes = temp.shape
    wide = nx + 2 * RIM
    tall = 2 * BASE + nz
    f32 = jnp.float32
    bonds = len(OFFSETS)
    scratch = (
        [pltpu.VMEM((n, wide, tall, lanes), f32) for n in PHASE_FIELDS]
        + [pltpu.VMEM((2, n, RIM * nx, lanes), f32) for n in PHASE_FIELDS]
        + [pltpu.VMEM((2, n, RIM * nx, lanes), f32) for n in PHASE_FIELDS]
        + [pltpu.VMEM((2, 2, n, 16, lanes), f32) for n in PHASE_FIELDS]
        + [pltpu.VMEM(tally.shape, jnp.int32), pltpu.VMEM(sites.shape, jnp.int32)]
        + [pltpu.VMEM((wide, tall, lanes), f32)] * 4
        + [pltpu.VMEM((2, nx, nz, lanes), f32)]
        + [pltpu.VMEM((nx, nz, lanes), f32)] * 4
        + [pltpu.VMEM((3, nx, nz, lanes), f32)] * 2
        + [pltpu.VMEM((nx, bonds, 3, nz, lanes), f32), pltpu.VMEM((nx, bonds, nz, lanes), f32)]
        + [
            pltpu.SemaphoreType.DMA((5,)),
            pltpu.SemaphoreType.DMA((4, len(DIRECTIONS))),
            pltpu.SemaphoreType.DMA((4, len(DIRECTIONS))),
        ]
    )
    return pl.pallas_call(
        kernel,
        out_shape=(
            jax.ShapeDtypeStruct(temp.shape, f32),
            jax.ShapeDtypeStruct(shift.shape, f32),
        ),
        in_specs=[pl.BlockSpec(memory_space=pl.ANY)] * 5,
        out_specs=(
            pl.BlockSpec(memory_space=pl.ANY),
            pl.BlockSpec(memory_space=pltpu.VMEM),
        ),
        scratch_shapes=scratch,
        compiler_params=pltpu.CompilerParams(
            collective_id=0, has_side_effects=True, vmem_limit_bytes=40 * 2**20
        ),
    )(temp, cond, shift, tally, sites)


def solution(mesh):
    return jax.shard_map(
        per_device,
        mesh=mesh,
        in_specs=(
            P(("parts", "lat", "sub"), "height", None),
            P(("parts", "lat", "sub"), "height", None),
            P(None, ("parts", "lat", "sub"), "height", None),
            P("parts", None),
            P("parts", None),
        ),
        out_specs=(
            P(("parts", "lat", "sub"), "height", None),
            P(None, ("parts", "lat", "sub"), "height", None),
        ),
        check_vma=False,
    )
```

```python
import functools
import math

import jax
import jax.numpy as jnp
from jax import lax
from jax.experimental import pallas as pl
from jax.experimental.pallas import tpu as pltpu
from jax.sharding import PartitionSpec as P

laser_energy_input = 1.5
thermal_swelling = 0.01
pressure_coef = -10.0
stiffness_coef = 300.0

RIM = 3
REACH = RIM * RIM
BASE = 8

OFFSETS = [
    (a, b, c)
    for c in range(-RIM, RIM + 1)
    for a in range(-RIM, RIM + 1)
    for b in range(-RIM, RIM + 1)
    if 0 < a * a + b * b + c * c <= REACH
]
PLANE = [
    (a, b)
    for a in range(-RIM, RIM + 1)
    for b in range(-RIM, RIM + 1)
    if a * a + b * b <= REACH
]
SQUARES = sorted({a * a + b * b for a, b in PLANE})
TOTAL_WEIGHT = sum(1.0 / math.sqrt(a * a + b * b + c * c) for a, b, c in OFFSETS)
DIRECTIONS = [(dx, dz) for dx in (-1, 0, 1) for dz in (-1, 0, 1) if (dx, dz) != (0, 0)]
PHASE_FIELDS = (2, 3, 2, 1, 1)
VMEM_BYTES = 63 * 2**20


def inverse_distance(square):
    return 1.0 / math.sqrt(square)


def kernel(
    temp_in,
    cond_in,
    shift_in,
    tally_in,
    sites_in,
    temp_out,
    force_out,
    e0,
    e1,
    e2,
    e3,
    e4,
    p0,
    p1,
    p2,
    p3,
    p4,
    z0,
    z1,
    z2,
    z3,
    z4,
    c0,
    c1,
    c2,
    c3,
    c4,
    tally,
    sites,
    act,
    act_k,
    act_t,
    act_kt,
    warmth,
    source,
    sum_a,
    sum_ak,
    vol,
    dil,
    total,
    normal,
    strain,
    local_sem,
    send_sem,
    recv_sem,
):
    nx, nz, lanes = temp_in.shape
    across_total = tally_in.shape[0]
    n_sub = lax.axis_size("sub")
    n_lateral = lax.axis_size("lat") * n_sub
    n_height = lax.axis_size("height")
    total_z = n_height * nz
    at_x = lax.axis_index("lat") * n_sub + lax.axis_index("sub")
    at_z = lax.axis_index("height")
    start_x = at_x * nx
    start_z = at_z * nz
    own_x = slice(RIM, RIM + nx)
    own_z = slice(BASE, BASE + nz)
    ext, packed = (e0, e1, e2, e3, e4), (p0, p1, p2, p3, p4)
    faces, corners = (z0, z1, z2, z3, z4), (c0, c1, c2, c3, c4)
    phases = len(PHASE_FIELDS)

    def exists(dx, dz):
        result = None
        for step, at, count in ((dx, at_x, n_lateral), (dz, at_z, n_height)):
            if step:
                test = at + step >= 0 if step < 0 else at + step < count
                result = test if result is None else jnp.logical_and(result, test)
        return result

    def device(dx, dz):
        to_x = at_x + dx
        return {"lat": to_x // n_sub, "sub": to_x % n_sub, "height": at_z + dz}

    def message(phase, which):
        dx, dz = DIRECTIONS[which]
        if dz == 0:
            here = slice(RIM, 2 * RIM) if dx < 0 else slice(nx, RIM + nx)
            there = slice(RIM + nx, 2 * RIM + nx) if dx < 0 else slice(0, RIM)
            src = ext[phase].at[:, here, own_z]
            dst = ext[phase].at[:, there, own_z]
        else:
            side, far = (0, 1) if dz < 0 else (1, 0)
            if dx == 0:
                src, dst = packed[phase].at[side], faces[phase].at[far]
            else:
                rows = slice(0, 16) if dx < 0 else slice(RIM * nx - 16, RIM * nx)
                src = packed[phase].at[side, :, rows]
                dst = corners[phase].at[far, 1 if dx < 0 else 0]
        return pltpu.make_async_remote_copy(
            src_ref=src,
            dst_ref=dst,
            send_sem=send_sem.at[phase, which],
            recv_sem=recv_sem.at[phase, which],
            device_id=device(dx, dz),
            device_id_type=pl.DeviceIdType.MESH,
        )

    def pack(phase):
        for f in range(PHASE_FIELDS[phase]):
            for x in range(nx):
                tile = ext[phase][f, RIM + x, own_z, :]
                packed[phase][0, f, RIM * x : RIM * x + RIM, :] = tile[0:RIM]
                packed[phase][1, f, RIM * x : RIM * x + RIM, :] = tile[nz - RIM : nz]

    def send(phase):
        for which, (dx, dz) in enumerate(DIRECTIONS):

            @pl.when(exists(dx, dz))
            def _(which=which):
                message(phase, which).start()

    def receive(phase):
        for which, (dx, dz) in enumerate(DIRECTIONS):

            @pl.when(exists(-dx, -dz))
            def _(which=which):
                message(phase, which).wait_recv()

        for f in range(PHASE_FIELDS[phase]):
            for side in range(2):
                rows = slice(BASE - RIM, BASE) if side == 0 else slice(BASE + nz, BASE + nz + RIM)
                for x in range(nx):
                    ext[phase][f, RIM + x, rows, :] = faces[phase][side, f, RIM * x : RIM * x + RIM, :]
                for i in range(RIM):
                    low = 16 - REACH + RIM * i
                    ext[phase][f, i, rows, :] = corners[phase][side, 0, f, low : low + RIM, :]
                    ext[phase][f, RIM + nx + i, rows, :] = corners[phase][
                        side, 1, f, RIM * i : RIM * i + RIM, :
                    ]

    loads = [
        pltpu.make_async_copy(temp_in, e0.at[0, own_x, own_z], local_sem.at[0]),
        pltpu.make_async_copy(cond_in, e0.at[1, own_x, own_z], local_sem.at[1]),
        pltpu.make_async_copy(shift_in, e1.at[:, own_x, own_z], local_sem.at[2]),
        pltpu.make_async_copy(tally_in, tally, local_sem.at[3]),
        pltpu.make_async_copy(sites_in, sites, local_sem.at[4]),
    ]
    for load in loads:
        load.start()

    for phase in range(phases):
        for f in range(PHASE_FIELDS[phase]):
            zeros = jnp.zeros((RIM, nz, lanes), jnp.float32)
            ext[phase][f, 0:RIM, own_z, :] = zeros
            ext[phase][f, RIM + nx : 2 * RIM + nx, own_z, :] = zeros
        faces[phase][...] = jnp.zeros_like(faces[phase])
        corners[phase][...] = jnp.zeros_like(corners[phase])

    barrier = pltpu.get_barrier_semaphore()
    for dx, dz in DIRECTIONS:

        @pl.when(exists(dx, dz))
        def _(dx=dx, dz=dz):
            pl.semaphore_signal(
                barrier, inc=1, device_id=device(dx, dz), device_id_type=pl.DeviceIdType.MESH
            )

    for load in loads[:2]:
        load.wait()
    pack(0)
    beside = jnp.where(at_x > 0, 1, 0) + jnp.where(at_x + 1 < n_lateral, 1, 0)
    stacked = jnp.where(at_z > 0, 1, 0) + jnp.where(at_z + 1 < n_height, 1, 0)
    pl.semaphore_wait(barrier, (beside + 1) * (stacked + 1) - 1)

    send(0)
    loads[2].wait()
    pack(1)
    send(1)

    lane = lax.broadcasted_iota(jnp.int32, (nz, lanes), 1)

    def frame(value, c):
        return value if c == 0 else pltpu.roll(value, c % lanes, 1)

    def unframe(value, c):
        if c == 0:
            return value
        inside = lane < lanes - c if c > 0 else lane >= -c
        return jnp.where(inside, pltpu.roll(value, (-c) % lanes, 1), 0.0)

    def near(ref, x, a, b):
        return ref[x + (RIM + a), BASE + b : BASE + b + nz, :]

    def ring_sums(ref, x):
        sums = {}
        for a, b in PLANE:
            square = a * a + b * b
            value = near(ref, x, a, b)
            sums[square] = sums[square] + value if square in sums else value
        return sums

    def weighted(sums, weight):
        result = None
        for c in range(RIM + 1):
            part = None
            for square in SQUARES:
                if 0 < square + c * c <= REACH:
                    term = sums[square] * weight(square + c * c)
                    part = term if part is None else part + term
            for sign in (1, -1) if c else (1,):
                moved = unframe(part, sign * c)
                result = moved if result is None else result + moved
        return result

    for load in loads[3:]:
        load.wait()
    heights = start_z - BASE + lax.broadcasted_iota(jnp.int32, (act.shape[1], lanes), 0)
    for x in range(nx + 2 * RIM):
        line = start_x + (x - RIM)
        count = tally[pl.ds(jnp.clip(line, 0, across_total - 1), 1), :]
        count = jnp.where(jnp.logical_and(line >= 0, line < across_total), count, 0)
        act[x] = jnp.where((heights >= 0) & (heights < count), 1.0, 0.0)

    for step in range(2):
        spots = sites[step : step + 1, :]
        n_spots = spots.shape[1]
        rows = []
        for x in range(nx):
            level = start_z + lax.broadcasted_iota(jnp.int32, (nz, n_spots), 0)
            gap = spots - ((start_x + x) * total_z + level) * lanes
            rows.append(jnp.where((gap >= 0) & (gap < lanes), 1.0, 0.0))
        row_hit = jnp.concatenate(rows, 0)
        lane_hit = jnp.where(
            lax.broadcasted_iota(jnp.int32, (lanes, n_spots), 0) == lax.rem(spots, lanes), 1.0, 0.0
        )
        hits = lax.dot_general(
            row_hit, lane_hit, (((1,), (1,)), ((), ())), preferred_element_type=jnp.float32
        )
        source[step] = hits.reshape(nx, nz, lanes)

    @pl.loop(0, nx)
    def _(x):
        sums = ring_sums(act, x)
        sum_a[x] = weighted(sums, inverse_distance)
        mass = weighted(sums, math.sqrt)
        mass = jnp.where(near(act, x, 0, 0) > 0, mass, 1.0)
        vol[x] = mass
        e2[1, x + RIM, own_z, :] = stiffness_coef / mass

    receive(0)

    def heat(field, step, x):
        rate_t = weighted(ring_sums(act_t, x), inverse_distance)
        rate_kt = weighted(ring_sums(act_kt, x), inverse_distance)
        temp = near(field, x, 0, 0)
        cond = near(e0.at[1], x, 0, 0)
        flow = cond * rate_t + rate_kt - temp * (cond * sum_a[x] + sum_ak[x])
        return temp + near(act, x, 0, 0) * (
            flow * (0.5 / TOTAL_WEIGHT) + laser_energy_input * source[step, x]
        )

    @pl.loop(0, nx + 2 * RIM)
    def _(x):
        act_k[x] = act[x] * e0[1, x]
        act_t[x] = act[x] * e0[0, x]
        act_kt[x] = act_k[x] * e0[0, x]

    @pl.loop(0, nx)
    def _(x):
        sum_ak[x] = weighted(ring_sums(act_k, x), inverse_distance)
        e2[0, x + RIM, own_z, :] = heat(e0.at[0], 0, x)

    pack(2)
    send(2)

    def geometry(x):
        centre = [near(e1.at[k], x, 0, 0) for k in range(3)]
        stretched = None
        bond = 0
        for c in range(-RIM, RIM + 1):
            moved = [frame(value, c) for value in centre]
            first = {a: moved[0] - float(a) for a in range(-RIM, RIM + 1)}
            second = {b: moved[1] - float(b) for b in range(-RIM, RIM + 1)}
            third = moved[2] - float(c)
            part = None
            for a, b, other in OFFSETS:
                if other != c:
                    continue
                separation = math.sqrt(a * a + b * b + c * c)
                d = (
                    near(e1.at[0], x, a, b) - first[a],
                    near(e1.at[1], x, a, b) - second[b],
                    near(e1.at[2], x, a, b) - third,
                )
                square = d[0] * d[0] + d[1] * d[1] + d[2] * d[2]
                inverse = lax.rsqrt(square)
                there = near(act, x, a, b)
                change = square * inverse - separation
                strain[x, bond] = change * (1.0 / separation)
                masked = inverse * there
                change = change * there
                part = change if part is None else part + change
                for k in range(3):
                    normal[x, bond, k] = d[k] * masked
                bond += 1
            part = unframe(part, c)
            stretched = part if stretched is None else stretched + part
        dil[x] = stretched

    half = nx // 2
    receive(1)

    @pl.loop(0, half)
    def _(x):
        geometry(x)

    receive(2)

    @pl.loop(0, nx + 2 * RIM)
    def _(x):
        act_t[x] = act[x] * e2[0, x]
        act_kt[x] = act_k[x] * e2[0, x]

    @pl.loop(0, nx)
    def _(x):
        warmed = heat(e2.at[0], 1, x)
        e3[0, x + RIM, own_z, :] = warmed
        temp_out[x] = warmed

    pack(3)
    send(3)

    @pl.loop(half, nx)
    def _(x):
        geometry(x)

    receive(3)

    @pl.loop(0, nx + 2 * RIM)
    def _(x):
        act_t[x] = act[x] * e3[0, x]
        warmth[x] = thermal_swelling * e3[0, x]

    @pl.loop(0, nx)
    def _(x):
        mass = vol[x]
        swell = weighted(ring_sums(act_t, x), math.sqrt) + near(e3.at[0], x, 0, 0) * mass
        change = near(act, x, 0, 0) * 3.0 * (dil[x] - thermal_swelling * swell) / mass
        e4[0, x + RIM, own_z, :] = pressure_coef * change / mass

    pack(4)
    send(4)

    @pl.loop(0, nx)
    def _(x):
        result = [None] * 3
        bond = 0
        for c in range(-RIM, RIM + 1):
            stiff = frame(near(e2.at[1], x, 0, 0), c)
            warm = frame(near(warmth, x, 0, 0), c)
            parts = [None] * 3
            for a, b, other in OFFSETS:
                if other != c:
                    continue
                swell = warm + near(warmth, x, a, b)
                scale = (stiff + near(e2.at[1], x, a, b)) * (strain[x, bond] - swell)
                for k in range(3):
                    term = normal[x, bond, k] * scale
                    parts[k] = term if parts[k] is None else parts[k] + term
                bond += 1
            for k in range(3):
                moved = unframe(parts[k], c)
                result[k] = moved if result[k] is None else result[k] + moved
        for k in range(3):
            total[k, x] = result[k]

    receive(4)

    @pl.loop(0, nx)
    def _(x):
        pressure = near(e4.at[0], x, 0, 0)
        result = [total[k, x] for k in range(3)]
        bond = 0
        for c in range(-RIM, RIM + 1):
            own = frame(pressure, c)
            parts = [None] * 3
            for a, b, other in OFFSETS:
                if other != c:
                    continue
                push = own + near(e4.at[0], x, a, b)
                for k in range(3):
                    term = normal[x, bond, k] * push
                    parts[k] = term if parts[k] is None else parts[k] + term
                bond += 1
            for k in range(3):
                result[k] = result[k] + unframe(parts[k], c)
        for k in range(3):
            force_out[k, x] = near(act, x, 0, 0) * result[k]

    for phase in range(phases):
        for which, (dx, dz) in enumerate(DIRECTIONS):

            @pl.when(exists(dx, dz))
            def _(phase=phase, which=which):
                message(phase, which).wait_send()


def hand_over(temp, force, temp_out, force_out, sem):
    copies = [
        pltpu.make_async_copy(temp, temp_out, sem.at[0]),
        pltpu.make_async_copy(force, force_out, sem.at[1]),
    ]
    for copy in copies:
        copy.start()
    for copy in copies:
        copy.wait()


def per_device(temp, cond, shift, tally, sites):
    nx, nz, lanes = temp.shape
    wide = nx + 2 * RIM
    tall = 2 * BASE + nz
    f32 = jnp.float32
    bonds = len(OFFSETS)
    scratch = (
        [pltpu.VMEM((n, wide, tall, lanes), f32) for n in PHASE_FIELDS]
        + [pltpu.VMEM((2, n, RIM * nx, lanes), f32) for n in PHASE_FIELDS]
        + [pltpu.VMEM((2, n, RIM * nx, lanes), f32) for n in PHASE_FIELDS]
        + [pltpu.VMEM((2, 2, n, 16, lanes), f32) for n in PHASE_FIELDS]
        + [pltpu.VMEM(tally.shape, jnp.int32), pltpu.VMEM(sites.shape, jnp.int32)]
        + [pltpu.VMEM((wide, tall, lanes), f32)] * 5
        + [pltpu.VMEM((2, nx, nz, lanes), f32)]
        + [pltpu.VMEM((nx, nz, lanes), f32)] * 4
        + [pltpu.VMEM((3, nx, nz, lanes), f32)]
        + [pltpu.VMEM((nx, bonds, 3, nz, lanes), f32), pltpu.VMEM((nx, bonds, nz, lanes), f32)]
        + [
            pltpu.SemaphoreType.DMA((5,)),
            pltpu.SemaphoreType.DMA((len(PHASE_FIELDS), len(DIRECTIONS))),
            pltpu.SemaphoreType.DMA((len(PHASE_FIELDS), len(DIRECTIONS))),
        ]
    )
    whole = pl.BlockSpec(memory_space=pltpu.VMEM)
    results = pl.pallas_call(
        kernel,
        out_shape=(pltpu.VMEM(temp.shape, f32), pltpu.VMEM(shift.shape, f32)),
        in_specs=[pl.BlockSpec(memory_space=pl.ANY)] * 5,
        out_specs=(whole, whole),
        scratch_shapes=scratch,
        compiler_params=pltpu.CompilerParams(
            collective_id=0, has_side_effects=True, vmem_limit_bytes=VMEM_BYTES
        ),
    )(temp, cond, shift, tally, sites)
    return pl.pallas_call(
        hand_over,
        out_shape=(
            jax.ShapeDtypeStruct(temp.shape, f32),
            jax.ShapeDtypeStruct(shift.shape, f32),
        ),
        in_specs=[pl.BlockSpec(memory_space=pl.ANY)] * 2,
        out_specs=(pl.BlockSpec(memory_space=pl.ANY),) * 2,
        scratch_shapes=[pltpu.SemaphoreType.DMA((2,))],
    )(*results)


def solution(mesh):
    return jax.shard_map(
        per_device,
        mesh=mesh,
        in_specs=(
            P(("parts", "lat", "sub"), "height", None),
            P(("parts", "lat", "sub"), "height", None),
            P(None, ("parts", "lat", "sub"), "height", None),
            P("parts", None),
            P("parts", None),
        ),
        out_specs=(
            P(("parts", "lat", "sub"), "height", None),
            P(None, ("parts", "lat", "sub"), "height", None),
        ),
        check_vma=False,
    )
```

```python
import functools
import math

import jax
import jax.numpy as jnp
from jax import lax
from jax.experimental import pallas as pl
from jax.experimental.pallas import tpu as pltpu
from jax.sharding import PartitionSpec as P

laser_energy_input = 1.5
thermal_swelling = 0.01
pressure_coef = -10.0
stiffness_coef = 300.0

RIM = 3
REACH = RIM * RIM
BASE = 8

OFFSETS = [
    (a, b, c)
    for c in range(-RIM, RIM + 1)
    for a in range(-RIM, RIM + 1)
    for b in range(-RIM, RIM + 1)
    if 0 < a * a + b * b + c * c <= REACH
]
PLANE = [
    (a, b)
    for a in range(-RIM, RIM + 1)
    for b in range(-RIM, RIM + 1)
    if a * a + b * b <= REACH
]
SQUARES = sorted({a * a + b * b for a, b in PLANE})
TOTAL_WEIGHT = sum(1.0 / math.sqrt(a * a + b * b + c * c) for a, b, c in OFFSETS)
DIRECTIONS = [(dx, dz) for dx in (-1, 0, 1) for dz in (-1, 0, 1) if (dx, dz) != (0, 0)]
PHASE_FIELDS = (2, 3, 2, 1, 1)
VMEM_BYTES = 63 * 2**20


def inverse_distance(square):
    return 1.0 / math.sqrt(square)


def kernel(
    temp_in,
    cond_in,
    shift_in,
    tally_in,
    sites_in,
    temp_out,
    force_out,
    e0,
    e1,
    e2,
    e3,
    e4,
    p0,
    p1,
    p2,
    p3,
    p4,
    z0,
    z1,
    z2,
    z3,
    z4,
    c0,
    c1,
    c2,
    c3,
    c4,
    tally,
    sites,
    act,
    act_k,
    act_t,
    act_kt,
    warmth,
    source,
    sum_a,
    sum_ak,
    vol,
    dil,
    total,
    normal,
    strain,
    local_sem,
    send_sem,
    recv_sem,
):
    nx, nz, lanes = temp_in.shape
    across_total = tally_in.shape[0]
    n_sub = lax.axis_size("sub")
    n_lateral = lax.axis_size("lat") * n_sub
    n_height = lax.axis_size("height")
    total_z = n_height * nz
    at_x = lax.axis_index("lat") * n_sub + lax.axis_index("sub")
    at_z = lax.axis_index("height")
    start_x = at_x * nx
    start_z = at_z * nz
    own_x = slice(RIM, RIM + nx)
    own_z = slice(BASE, BASE + nz)
    ext, packed = (e0, e1, e2, e3, e4), (p0, p1, p2, p3, p4)
    faces, corners = (z0, z1, z2, z3, z4), (c0, c1, c2, c3, c4)
    phases = len(PHASE_FIELDS)

    def exists(dx, dz):
        result = None
        for step, at, count in ((dx, at_x, n_lateral), (dz, at_z, n_height)):
            if step:
                test = at + step >= 0 if step < 0 else at + step < count
                result = test if result is None else jnp.logical_and(result, test)
        return result

    def device(dx, dz):
        to_x = at_x + dx
        return {"lat": to_x // n_sub, "sub": to_x % n_sub, "height": at_z + dz}

    def message(phase, which):
        dx, dz = DIRECTIONS[which]
        if dz == 0:
            here = slice(RIM, 2 * RIM) if dx < 0 else slice(nx, RIM + nx)
            there = slice(RIM + nx, 2 * RIM + nx) if dx < 0 else slice(0, RIM)
            src = ext[phase].at[:, here, own_z]
            dst = ext[phase].at[:, there, own_z]
        else:
            side, far = (0, 1) if dz < 0 else (1, 0)
            if dx == 0:
                src, dst = packed[phase].at[side], faces[phase].at[far]
            else:
                rows = slice(0, 16) if dx < 0 else slice(RIM * nx - 16, RIM * nx)
                src = packed[phase].at[side, :, rows]
                dst = corners[phase].at[far, 1 if dx < 0 else 0]
        return pltpu.make_async_remote_copy(
            src_ref=src,
            dst_ref=dst,
            send_sem=send_sem.at[phase, which],
            recv_sem=recv_sem.at[phase, which],
            device_id=device(dx, dz),
            device_id_type=pl.DeviceIdType.MESH,
        )

    def pack(phase):
        for f in range(PHASE_FIELDS[phase]):
            for x in range(nx):
                tile = ext[phase][f, RIM + x, own_z, :]
                packed[phase][0, f, RIM * x : RIM * x + RIM, :] = tile[0:RIM]
                packed[phase][1, f, RIM * x : RIM * x + RIM, :] = tile[nz - RIM : nz]

    def send(phase):
        for which, (dx, dz) in enumerate(DIRECTIONS):

            @pl.when(exists(dx, dz))
            def _(which=which):
                message(phase, which).start()

    def receive(phase):
        for which, (dx, dz) in enumerate(DIRECTIONS):

            @pl.when(exists(-dx, -dz))
            def _(which=which):
                message(phase, which).wait_recv()

        for f in range(PHASE_FIELDS[phase]):
            for side in range(2):
                rows = slice(BASE - RIM, BASE) if side == 0 else slice(BASE + nz, BASE + nz + RIM)
                for x in range(nx):
                    ext[phase][f, RIM + x, rows, :] = faces[phase][side, f, RIM * x : RIM * x + RIM, :]
                for i in range(RIM):
                    low = 16 - REACH + RIM * i
                    ext[phase][f, i, rows, :] = corners[phase][side, 0, f, low : low + RIM, :]
                    ext[phase][f, RIM + nx + i, rows, :] = corners[phase][
                        side, 1, f, RIM * i : RIM * i + RIM, :
                    ]

    loads = [
        pltpu.make_async_copy(temp_in, e0.at[0, own_x, own_z], local_sem.at[0]),
        pltpu.make_async_copy(cond_in, e0.at[1, own_x, own_z], local_sem.at[1]),
        pltpu.make_async_copy(shift_in, e1.at[:, own_x, own_z], local_sem.at[2]),
        pltpu.make_async_copy(tally_in, tally, local_sem.at[3]),
        pltpu.make_async_copy(sites_in, sites, local_sem.at[4]),
    ]
    for load in loads:
        load.start()

    for phase in range(phases):
        for f in range(PHASE_FIELDS[phase]):
            zeros = jnp.zeros((RIM, nz, lanes), jnp.float32)
            ext[phase][f, 0:RIM, own_z, :] = zeros
            ext[phase][f, RIM + nx : 2 * RIM + nx, own_z, :] = zeros
        faces[phase][...] = jnp.zeros_like(faces[phase])
        corners[phase][...] = jnp.zeros_like(corners[phase])

    barrier = pltpu.get_barrier_semaphore()
    for dx, dz in DIRECTIONS:

        @pl.when(exists(dx, dz))
        def _(dx=dx, dz=dz):
            pl.semaphore_signal(
                barrier, inc=1, device_id=device(dx, dz), device_id_type=pl.DeviceIdType.MESH
            )

    for load in loads[:2]:
        load.wait()
    pack(0)
    beside = jnp.where(at_x > 0, 1, 0) + jnp.where(at_x + 1 < n_lateral, 1, 0)
    stacked = jnp.where(at_z > 0, 1, 0) + jnp.where(at_z + 1 < n_height, 1, 0)
    pl.semaphore_wait(barrier, (beside + 1) * (stacked + 1) - 1)

    send(0)
    loads[2].wait()
    pack(1)
    send(1)

    lane = lax.broadcasted_iota(jnp.int32, (nz, lanes), 1)

    def frame(value, c):
        return value if c == 0 else pltpu.roll(value, c % lanes, 1)

    def unframe(value, c):
        if c == 0:
            return value
        inside = lane < lanes - c if c > 0 else lane >= -c
        return jnp.where(inside, pltpu.roll(value, (-c) % lanes, 1), 0.0)

    def near(ref, x, a, b):
        return ref[x + (RIM + a), BASE + b : BASE + b + nz, :]

    def ring_sums(ref, x):
        sums = {}
        for a, b in PLANE:
            square = a * a + b * b
            value = near(ref, x, a, b)
            sums[square] = sums[square] + value if square in sums else value
        return sums

    def weighted(sums, weight):
        result = None
        for c in range(RIM + 1):
            part = None
            for square in SQUARES:
                if 0 < square + c * c <= REACH:
                    term = sums[square] * weight(square + c * c)
                    part = term if part is None else part + term
            for sign in (1, -1) if c else (1,):
                moved = unframe(part, sign * c)
                result = moved if result is None else result + moved
        return result

    for load in loads[3:]:
        load.wait()
    heights = start_z - BASE + lax.broadcasted_iota(jnp.int32, (act.shape[1], lanes), 0)
    for x in range(nx + 2 * RIM):
        line = start_x + (x - RIM)
        count = tally[pl.ds(jnp.clip(line, 0, across_total - 1), 1), :]
        count = jnp.where(jnp.logical_and(line >= 0, line < across_total), count, 0)
        act[x] = jnp.where((heights >= 0) & (heights < count), 1.0, 0.0)

    for step in range(2):
        spots = sites[step : step + 1, :]
        n_spots = spots.shape[1]
        rows = []
        for x in range(nx):
            level = start_z + lax.broadcasted_iota(jnp.int32, (nz, n_spots), 0)
            gap = spots - ((start_x + x) * total_z + level) * lanes
            rows.append(jnp.where((gap >= 0) & (gap < lanes), 1.0, 0.0))
        row_hit = jnp.concatenate(rows, 0)
        lane_hit = jnp.where(
            lax.broadcasted_iota(jnp.int32, (lanes, n_spots), 0) == lax.rem(spots, lanes), 1.0, 0.0
        )
        hits = lax.dot_general(
            row_hit, lane_hit, (((1,), (1,)), ((), ())), preferred_element_type=jnp.float32
        )
        source[step] = hits.reshape(nx, nz, lanes)

    @pl.loop(0, nx)
    def _(x):
        sums = ring_sums(act, x)
        sum_a[x] = weighted(sums, inverse_distance)
        mass = weighted(sums, math.sqrt)
        mass = jnp.where(near(act, x, 0, 0) > 0, mass, 1.0)
        vol[x] = mass
        e2[1, x + RIM, own_z, :] = stiffness_coef / mass

    receive(0)

    def heat(field, step, x):
        rate_t = weighted(ring_sums(act_t, x), inverse_distance)
        rate_kt = weighted(ring_sums(act_kt, x), inverse_distance)
        temp = near(field, x, 0, 0)
        cond = near(e0.at[1], x, 0, 0)
        flow = cond * rate_t + rate_kt - temp * (cond * sum_a[x] + sum_ak[x])
        return temp + near(act, x, 0, 0) * (
            flow * (0.5 / TOTAL_WEIGHT) + laser_energy_input * source[step, x]
        )

    @pl.loop(0, nx + 2 * RIM)
    def _(x):
        act_k[x] = act[x] * e0[1, x]
        act_t[x] = act[x] * e0[0, x]
        act_kt[x] = act_k[x] * e0[0, x]

    @pl.loop(0, nx)
    def _(x):
        sum_ak[x] = weighted(ring_sums(act_k, x), inverse_distance)
        e2[0, x + RIM, own_z, :] = heat(e0.at[0], 0, x)

    pack(2)
    send(2)

    def geometry(x):
        centre = [near(e1.at[k], x, 0, 0) for k in range(3)]
        stretched = None
        bond = 0
        for c in range(-RIM, RIM + 1):
            moved = [frame(value, c) for value in centre]
            first = {a: moved[0] - float(a) for a in range(-RIM, RIM + 1)}
            second = {b: moved[1] - float(b) for b in range(-RIM, RIM + 1)}
            third = moved[2] - float(c)
            part = None
            for a, b, other in OFFSETS:
                if other != c:
                    continue
                separation = math.sqrt(a * a + b * b + c * c)
                d = (
                    near(e1.at[0], x, a, b) - first[a],
                    near(e1.at[1], x, a, b) - second[b],
                    near(e1.at[2], x, a, b) - third,
                )
                square = d[0] * d[0] + d[1] * d[1] + d[2] * d[2]
                inverse = lax.rsqrt(square)
                there = near(act, x, a, b)
                change = square * inverse - separation
                strain[x, bond] = change * (1.0 / separation)
                masked = inverse * there
                change = change * there
                part = change if part is None else part + change
                for k in range(3):
                    normal[x, bond, k] = d[k] * masked
                bond += 1
            part = unframe(part, c)
            stretched = part if stretched is None else stretched + part
        dil[x] = stretched

    half = nx // 2
    receive(1)

    @pl.loop(0, half)
    def _(x):
        geometry(x)

    receive(2)

    @pl.loop(0, nx + 2 * RIM)
    def _(x):
        act_t[x] = act[x] * e2[0, x]
        act_kt[x] = act_k[x] * e2[0, x]

    @pl.loop(0, nx)
    def _(x):
        warmed = heat(e2.at[0], 1, x)
        e3[0, x + RIM, own_z, :] = warmed
        temp_out[x] = warmed

    pack(3)
    send(3)

    @pl.loop(half, nx)
    def _(x):
        geometry(x)

    receive(3)

    @pl.loop(0, nx + 2 * RIM)
    def _(x):
        act_t[x] = act[x] * e3[0, x]
        warmth[x] = thermal_swelling * e3[0, x]

    @pl.loop(0, nx)
    def _(x):
        mass = vol[x]
        swell = weighted(ring_sums(act_t, x), math.sqrt) + near(e3.at[0], x, 0, 0) * mass
        change = near(act, x, 0, 0) * 3.0 * (dil[x] - thermal_swelling * swell) / mass
        e4[0, x + RIM, own_z, :] = pressure_coef * change / mass

    pack(4)
    send(4)

    @pl.loop(0, nx)
    def _(x):
        result = [None] * 3
        bond = 0
        for c in range(-RIM, RIM + 1):
            stiff = frame(near(e2.at[1], x, 0, 0), c)
            warm = frame(near(warmth, x, 0, 0), c)
            parts = [None] * 3
            for a, b, other in OFFSETS:
                if other != c:
                    continue
                swell = warm + near(warmth, x, a, b)
                scale = (stiff + near(e2.at[1], x, a, b)) * (strain[x, bond] - swell)
                for k in range(3):
                    term = normal[x, bond, k] * scale
                    parts[k] = term if parts[k] is None else parts[k] + term
                bond += 1
            for k in range(3):
                moved = unframe(parts[k], c)
                result[k] = moved if result[k] is None else result[k] + moved
        for k in range(3):
            total[k, x] = result[k]

    receive(4)

    @pl.loop(0, nx)
    def _(x):
        pressure = near(e4.at[0], x, 0, 0)
        result = [total[k, x] for k in range(3)]
        bond = 0
        for c in range(-RIM, RIM + 1):
            own = frame(pressure, c)
            parts = [None] * 3
            for a, b, other in OFFSETS:
                if other != c:
                    continue
                push = own + near(e4.at[0], x, a, b)
                for k in range(3):
                    term = normal[x, bond, k] * push
                    parts[k] = term if parts[k] is None else parts[k] + term
                bond += 1
            for k in range(3):
                result[k] = result[k] + unframe(parts[k], c)
        for k in range(3):
            force_out[k, x] = near(act, x, 0, 0) * result[k]

    for phase in range(phases):
        for which, (dx, dz) in enumerate(DIRECTIONS):

            @pl.when(exists(dx, dz))
            def _(phase=phase, which=which):
                message(phase, which).wait_send()


def per_device(temp, cond, shift, tally, sites):
    nx, nz, lanes = temp.shape
    wide = nx + 2 * RIM
    tall = 2 * BASE + nz
    f32 = jnp.float32
    bonds = len(OFFSETS)
    scratch = (
        [pltpu.VMEM((n, wide, tall, lanes), f32) for n in PHASE_FIELDS]
        + [pltpu.VMEM((2, n, RIM * nx, lanes), f32) for n in PHASE_FIELDS]
        + [pltpu.VMEM((2, n, RIM * nx, lanes), f32) for n in PHASE_FIELDS]
        + [pltpu.VMEM((2, 2, n, 16, lanes), f32) for n in PHASE_FIELDS]
        + [pltpu.VMEM(tally.shape, jnp.int32), pltpu.VMEM(sites.shape, jnp.int32)]
        + [pltpu.VMEM((wide, tall, lanes), f32)] * 5
        + [pltpu.VMEM((2, nx, nz, lanes), f32)]
        + [pltpu.VMEM((nx, nz, lanes), f32)] * 4
        + [pltpu.VMEM((3, nx, nz, lanes), f32)]
        + [pltpu.VMEM((nx, bonds, 3, nz, lanes), f32), pltpu.VMEM((nx, bonds, nz, lanes), f32)]
        + [
            pltpu.SemaphoreType.DMA((5,)),
            pltpu.SemaphoreType.DMA((len(PHASE_FIELDS), len(DIRECTIONS))),
            pltpu.SemaphoreType.DMA((len(PHASE_FIELDS), len(DIRECTIONS))),
        ]
    )
    whole = pl.BlockSpec(memory_space=pltpu.VMEM)
    return pl.pallas_call(
        kernel,
        out_shape=(pltpu.VMEM(temp.shape, f32), pltpu.VMEM(shift.shape, f32)),
        in_specs=[pl.BlockSpec(memory_space=pl.ANY)] * 5,
        out_specs=(whole, whole),
        scratch_shapes=scratch,
        compiler_params=pltpu.CompilerParams(
            collective_id=0, has_side_effects=True, vmem_limit_bytes=VMEM_BYTES
        ),
    )(temp, cond, shift, tally, sites)


def solution(mesh):
    return jax.shard_map(
        per_device,
        mesh=mesh,
        in_specs=(
            P(("parts", "lat", "sub"), "height", None),
            P(("parts", "lat", "sub"), "height", None),
            P(None, ("parts", "lat", "sub"), "height", None),
            P("parts", None),
            P("parts", None),
        ),
        out_specs=(
            P(("parts", "lat", "sub"), "height", None),
            P(None, ("parts", "lat", "sub"), "height", None),
        ),
        check_vma=False,
    )
```

```python
import functools
import math

import jax
import jax.numpy as jnp
from jax import lax
from jax.experimental import pallas as pl
from jax.experimental.pallas import tpu as pltpu
from jax.sharding import PartitionSpec as P

laser_energy_input = 1.5
thermal_swelling = 0.01
pressure_coef = -10.0
stiffness_coef = 300.0

RIM = 3
REACH = RIM * RIM
BASE = 8

OFFSETS = [
    (a, b, c)
    for c in range(-RIM, RIM + 1)
    for a in range(-RIM, RIM + 1)
    for b in range(-RIM, RIM + 1)
    if 0 < a * a + b * b + c * c <= REACH
]
PLANE = [
    (a, b)
    for a in range(-RIM, RIM + 1)
    for b in range(-RIM, RIM + 1)
    if a * a + b * b <= REACH
]
SQUARES = sorted({a * a + b * b for a, b in PLANE})
TOTAL_WEIGHT = sum(1.0 / math.sqrt(a * a + b * b + c * c) for a, b, c in OFFSETS)
DIRECTIONS = [(dx, dz) for dx in (-1, 0, 1) for dz in (-1, 0, 1) if (dx, dz) != (0, 0)]
PHASE_FIELDS = (2, 3, 2, 1, 1)
VMEM_BYTES = 63 * 2**20


def inverse_distance(square):
    return 1.0 / math.sqrt(square)


def kernel(
    temp_in,
    cond_in,
    shift_in,
    tally_in,
    sites_in,
    temp_out,
    force_out,
    e0,
    e1,
    e2,
    e3,
    e4,
    p0,
    p1,
    p2,
    p3,
    p4,
    z0,
    z1,
    z2,
    z3,
    z4,
    c0,
    c1,
    c2,
    c3,
    c4,
    tally,
    sites,
    act,
    act_k,
    act_t,
    act_kt,
    warmth,
    source,
    sum_a,
    sum_ak,
    vol,
    dil,
    total,
    normal,
    strain,
    local_sem,
    send_sem,
    recv_sem,
):
    nx, nz, lanes = temp_in.shape
    across_total = tally_in.shape[0]
    n_sub = lax.axis_size("sub")
    n_lateral = lax.axis_size("lat") * n_sub
    n_height = lax.axis_size("height")
    total_z = n_height * nz
    at_x = lax.axis_index("lat") * n_sub + lax.axis_index("sub")
    at_z = lax.axis_index("height")
    start_x = at_x * nx
    start_z = at_z * nz
    own_x = slice(RIM, RIM + nx)
    own_z = slice(BASE, BASE + nz)
    ext, packed = (e0, e1, e2, e3, e4), (p0, p1, p2, p3, p4)
    faces, corners = (z0, z1, z2, z3, z4), (c0, c1, c2, c3, c4)
    phases = len(PHASE_FIELDS)

    def exists(dx, dz):
        result = None
        for step, at, count in ((dx, at_x, n_lateral), (dz, at_z, n_height)):
            if step:
                test = at + step >= 0 if step < 0 else at + step < count
                result = test if result is None else jnp.logical_and(result, test)
        return result

    def device(dx, dz):
        to_x = at_x + dx
        return {"lat": to_x // n_sub, "sub": to_x % n_sub, "height": at_z + dz}

    def message(phase, which):
        dx, dz = DIRECTIONS[which]
        if dz == 0:
            here = slice(RIM, 2 * RIM) if dx < 0 else slice(nx, RIM + nx)
            there = slice(RIM + nx, 2 * RIM + nx) if dx < 0 else slice(0, RIM)
            src = ext[phase].at[:, here, own_z]
            dst = ext[phase].at[:, there, own_z]
        else:
            side, far = (0, 1) if dz < 0 else (1, 0)
            if dx == 0:
                src, dst = packed[phase].at[side], faces[phase].at[far]
            else:
                rows = slice(0, 16) if dx < 0 else slice(RIM * nx - 16, RIM * nx)
                src = packed[phase].at[side, :, rows]
                dst = corners[phase].at[far, 1 if dx < 0 else 0]
        return pltpu.make_async_remote_copy(
            src_ref=src,
            dst_ref=dst,
            send_sem=send_sem.at[phase, which],
            recv_sem=recv_sem.at[phase, which],
            device_id=device(dx, dz),
            device_id_type=pl.DeviceIdType.MESH,
        )

    def pack(phase):
        for f in range(PHASE_FIELDS[phase]):
            for x in range(nx):
                tile = ext[phase][f, RIM + x, own_z, :]
                packed[phase][0, f, RIM * x : RIM * x + RIM, :] = tile[0:RIM]
                packed[phase][1, f, RIM * x : RIM * x + RIM, :] = tile[nz - RIM : nz]

    def send(phase):
        for which, (dx, dz) in enumerate(DIRECTIONS):

            @pl.when(exists(dx, dz))
            def _(which=which):
                message(phase, which).start()

    def receive(phase):
        for which, (dx, dz) in enumerate(DIRECTIONS):

            @pl.when(exists(-dx, -dz))
            def _(which=which):
                message(phase, which).wait_recv()

        for f in range(PHASE_FIELDS[phase]):
            for side in range(2):
                rows = slice(BASE - RIM, BASE) if side == 0 else slice(BASE + nz, BASE + nz + RIM)
                for x in range(nx):
                    ext[phase][f, RIM + x, rows, :] = faces[phase][side, f, RIM * x : RIM * x + RIM, :]
                for i in range(RIM):
                    low = 16 - REACH + RIM * i
                    ext[phase][f, i, rows, :] = corners[phase][side, 0, f, low : low + RIM, :]
                    ext[phase][f, RIM + nx + i, rows, :] = corners[phase][
                        side, 1, f, RIM * i : RIM * i + RIM, :
                    ]

    loads = [
        pltpu.make_async_copy(temp_in, e0.at[0, own_x, own_z], local_sem.at[0]),
        pltpu.make_async_copy(cond_in, e0.at[1, own_x, own_z], local_sem.at[1]),
        pltpu.make_async_copy(shift_in, e1.at[:, own_x, own_z], local_sem.at[2]),
        pltpu.make_async_copy(tally_in, tally, local_sem.at[3]),
        pltpu.make_async_copy(sites_in, sites, local_sem.at[4]),
    ]
    for load in loads:
        load.start()

    for phase in range(phases):
        for f in range(PHASE_FIELDS[phase]):
            zeros = jnp.zeros((RIM, nz, lanes), jnp.float32)
            ext[phase][f, 0:RIM, own_z, :] = zeros
            ext[phase][f, RIM + nx : 2 * RIM + nx, own_z, :] = zeros
        faces[phase][...] = jnp.zeros_like(faces[phase])
        corners[phase][...] = jnp.zeros_like(corners[phase])

    barrier = pltpu.get_barrier_semaphore()
    for dx, dz in DIRECTIONS:

        @pl.when(exists(dx, dz))
        def _(dx=dx, dz=dz):
            pl.semaphore_signal(
                barrier, inc=1, device_id=device(dx, dz), device_id_type=pl.DeviceIdType.MESH
            )

    for load in loads[:2]:
        load.wait()
    pack(0)
    beside = jnp.where(at_x > 0, 1, 0) + jnp.where(at_x + 1 < n_lateral, 1, 0)
    stacked = jnp.where(at_z > 0, 1, 0) + jnp.where(at_z + 1 < n_height, 1, 0)
    pl.semaphore_wait(barrier, (beside + 1) * (stacked + 1) - 1)

    send(0)
    loads[2].wait()
    pack(1)
    send(1)

    lane = lax.broadcasted_iota(jnp.int32, (nz, lanes), 1)

    def frame(value, c):
        return value if c == 0 else pltpu.roll(value, c % lanes, 1)

    def unframe(value, c):
        if c == 0:
            return value
        inside = lane < lanes - c if c > 0 else lane >= -c
        return jnp.where(inside, pltpu.roll(value, (-c) % lanes, 1), 0.0)

    def near(ref, x, a, b):
        return ref[x + (RIM + a), BASE + b : BASE + b + nz, :]

    def ring_sums(ref, x):
        sums = {}
        for a, b in PLANE:
            square = a * a + b * b
            value = near(ref, x, a, b)
            sums[square] = sums[square] + value if square in sums else value
        return sums

    def weighted(sums, weight):
        result = None
        for c in range(RIM + 1):
            part = None
            for square in SQUARES:
                if 0 < square + c * c <= REACH:
                    term = sums[square] * weight(square + c * c)
                    part = term if part is None else part + term
            for sign in (1, -1) if c else (1,):
                moved = unframe(part, sign * c)
                result = moved if result is None else result + moved
        return result

    for load in loads[3:]:
        load.wait()
    heights = start_z - BASE + lax.broadcasted_iota(jnp.int32, (act.shape[1], lanes), 0)
    for x in range(nx + 2 * RIM):
        line = start_x + (x - RIM)
        count = tally[pl.ds(jnp.clip(line, 0, across_total - 1), 1), :]
        count = jnp.where(jnp.logical_and(line >= 0, line < across_total), count, 0)
        act[x] = jnp.where((heights >= 0) & (heights < count), 1.0, 0.0)

    for step in range(2):
        spots = sites[step : step + 1, :]
        n_spots = spots.shape[1]
        rows = []
        for x in range(nx):
            level = start_z + lax.broadcasted_iota(jnp.int32, (nz, n_spots), 0)
            gap = spots - ((start_x + x) * total_z + level) * lanes
            rows.append(jnp.where((gap >= 0) & (gap < lanes), 1.0, 0.0))
        row_hit = jnp.concatenate(rows, 0)
        lane_hit = jnp.where(
            lax.broadcasted_iota(jnp.int32, (lanes, n_spots), 0) == lax.rem(spots, lanes), 1.0, 0.0
        )
        hits = lax.dot_general(
            row_hit, lane_hit, (((1,), (1,)), ((), ())), preferred_element_type=jnp.float32
        )
        source[step] = hits.reshape(nx, nz, lanes)

    @pl.loop(0, nx, unroll=2)
    def _(x):
        sums = ring_sums(act, x)
        sum_a[x] = weighted(sums, inverse_distance)
        mass = weighted(sums, math.sqrt)
        mass = jnp.where(near(act, x, 0, 0) > 0, mass, 1.0)
        vol[x] = mass
        e2[1, x + RIM, own_z, :] = stiffness_coef / mass

    receive(0)

    def heat(field, step, x):
        rate_t = weighted(ring_sums(act_t, x), inverse_distance)
        rate_kt = weighted(ring_sums(act_kt, x), inverse_distance)
        temp = near(field, x, 0, 0)
        cond = near(e0.at[1], x, 0, 0)
        flow = cond * rate_t + rate_kt - temp * (cond * sum_a[x] + sum_ak[x])
        return temp + near(act, x, 0, 0) * (
            flow * (0.5 / TOTAL_WEIGHT) + laser_energy_input * source[step, x]
        )

    @pl.loop(0, nx + 2 * RIM, unroll=2)
    def _(x):
        act_k[x] = act[x] * e0[1, x]
        act_t[x] = act[x] * e0[0, x]
        act_kt[x] = act_k[x] * e0[0, x]

    @pl.loop(0, nx, unroll=2)
    def _(x):
        sum_ak[x] = weighted(ring_sums(act_k, x), inverse_distance)
        e2[0, x + RIM, own_z, :] = heat(e0.at[0], 0, x)

    pack(2)
    send(2)

    def geometry(x):
        centre = [near(e1.at[k], x, 0, 0) for k in range(3)]
        stretched = None
        bond = 0
        for c in range(-RIM, RIM + 1):
            moved = [frame(value, c) for value in centre]
            first = {a: moved[0] - float(a) for a in range(-RIM, RIM + 1)}
            second = {b: moved[1] - float(b) for b in range(-RIM, RIM + 1)}
            third = moved[2] - float(c)
            part = None
            for a, b, other in OFFSETS:
                if other != c:
                    continue
                separation = math.sqrt(a * a + b * b + c * c)
                d = (
                    near(e1.at[0], x, a, b) - first[a],
                    near(e1.at[1], x, a, b) - second[b],
                    near(e1.at[2], x, a, b) - third,
                )
                square = d[0] * d[0] + d[1] * d[1] + d[2] * d[2]
                inverse = lax.rsqrt(square)
                there = near(act, x, a, b)
                change = square * inverse - separation
                strain[x, bond] = change * (1.0 / separation)
                masked = inverse * there
                change = change * there
                part = change if part is None else part + change
                for k in range(3):
                    normal[x, bond, k] = d[k] * masked
                bond += 1
            part = unframe(part, c)
            stretched = part if stretched is None else stretched + part
        dil[x] = stretched

    half = nx // 2
    receive(1)

    @pl.loop(0, half)
    def _(x):
        geometry(x)

    receive(2)

    @pl.loop(0, nx + 2 * RIM, unroll=2)
    def _(x):
        act_t[x] = act[x] * e2[0, x]
        act_kt[x] = act_k[x] * e2[0, x]

    @pl.loop(0, nx, unroll=2)
    def _(x):
        warmed = heat(e2.at[0], 1, x)
        e3[0, x + RIM, own_z, :] = warmed
        temp_out[x] = warmed

    pack(3)
    send(3)

    @pl.loop(half, nx)
    def _(x):
        geometry(x)

    receive(3)

    @pl.loop(0, nx + 2 * RIM, unroll=2)
    def _(x):
        act_t[x] = act[x] * e3[0, x]
        warmth[x] = thermal_swelling * e3[0, x]

    @pl.loop(0, nx, unroll=2)
    def _(x):
        mass = vol[x]
        swell = weighted(ring_sums(act_t, x), math.sqrt) + near(e3.at[0], x, 0, 0) * mass
        change = near(act, x, 0, 0) * 3.0 * (dil[x] - thermal_swelling * swell) / mass
        e4[0, x + RIM, own_z, :] = pressure_coef * change / mass

    pack(4)
    send(4)

    @pl.loop(0, nx)
    def _(x):
        result = [None] * 3
        bond = 0
        for c in range(-RIM, RIM + 1):
            stiff = frame(near(e2.at[1], x, 0, 0), c)
            warm = frame(near(warmth, x, 0, 0), c)
            parts = [None] * 3
            for a, b, other in OFFSETS:
                if other != c:
                    continue
                swell = warm + near(warmth, x, a, b)
                scale = (stiff + near(e2.at[1], x, a, b)) * (strain[x, bond] - swell)
                for k in range(3):
                    term = normal[x, bond, k] * scale
                    parts[k] = term if parts[k] is None else parts[k] + term
                bond += 1
            for k in range(3):
                moved = unframe(parts[k], c)
                result[k] = moved if result[k] is None else result[k] + moved
        for k in range(3):
            total[k, x] = result[k]

    receive(4)

    @pl.loop(0, nx)
    def _(x):
        pressure = near(e4.at[0], x, 0, 0)
        result = [total[k, x] for k in range(3)]
        bond = 0
        for c in range(-RIM, RIM + 1):
            own = frame(pressure, c)
            parts = [None] * 3
            for a, b, other in OFFSETS:
                if other != c:
                    continue
                push = own + near(e4.at[0], x, a, b)
                for k in range(3):
                    term = normal[x, bond, k] * push
                    parts[k] = term if parts[k] is None else parts[k] + term
                bond += 1
            for k in range(3):
                result[k] = result[k] + unframe(parts[k], c)
        for k in range(3):
            force_out[k, x] = near(act, x, 0, 0) * result[k]

    for phase in range(phases):
        for which, (dx, dz) in enumerate(DIRECTIONS):

            @pl.when(exists(dx, dz))
            def _(phase=phase, which=which):
                message(phase, which).wait_send()


def per_device(temp, cond, shift, tally, sites):
    nx, nz, lanes = temp.shape
    wide = nx + 2 * RIM
    tall = 2 * BASE + nz
    f32 = jnp.float32
    bonds = len(OFFSETS)
    scratch = (
        [pltpu.VMEM((n, wide, tall, lanes), f32) for n in PHASE_FIELDS]
        + [pltpu.VMEM((2, n, RIM * nx, lanes), f32) for n in PHASE_FIELDS]
        + [pltpu.VMEM((2, n, RIM * nx, lanes), f32) for n in PHASE_FIELDS]
        + [pltpu.VMEM((2, 2, n, 16, lanes), f32) for n in PHASE_FIELDS]
        + [pltpu.VMEM(tally.shape, jnp.int32), pltpu.VMEM(sites.shape, jnp.int32)]
        + [pltpu.VMEM((wide, tall, lanes), f32)] * 5
        + [pltpu.VMEM((2, nx, nz, lanes), f32)]
        + [pltpu.VMEM((nx, nz, lanes), f32)] * 4
        + [pltpu.VMEM((3, nx, nz, lanes), f32)]
        + [pltpu.VMEM((nx, bonds, 3, nz, lanes), f32), pltpu.VMEM((nx, bonds, nz, lanes), f32)]
        + [
            pltpu.SemaphoreType.DMA((5,)),
            pltpu.SemaphoreType.DMA((len(PHASE_FIELDS), len(DIRECTIONS))),
            pltpu.SemaphoreType.DMA((len(PHASE_FIELDS), len(DIRECTIONS))),
        ]
    )
    whole = pl.BlockSpec(memory_space=pltpu.VMEM)
    return pl.pallas_call(
        kernel,
        out_shape=(pltpu.VMEM(temp.shape, f32), pltpu.VMEM(shift.shape, f32)),
        in_specs=[pl.BlockSpec(memory_space=pl.ANY)] * 5,
        out_specs=(whole, whole),
        scratch_shapes=scratch,
        compiler_params=pltpu.CompilerParams(
            collective_id=0, has_side_effects=True, vmem_limit_bytes=VMEM_BYTES
        ),
    )(temp, cond, shift, tally, sites)


def solution(mesh):
    return jax.shard_map(
        per_device,
        mesh=mesh,
        in_specs=(
            P(("parts", "lat", "sub"), "height", None),
            P(("parts", "lat", "sub"), "height", None),
            P(None, ("parts", "lat", "sub"), "height", None),
            P("parts", None),
            P("parts", None),
        ),
        out_specs=(
            P(("parts", "lat", "sub"), "height", None),
            P(None, ("parts", "lat", "sub"), "height", None),
        ),
        check_vma=False,
    )
```
